32 devices in a mesh: comp: 4 (over z), space: 8 (over y, x, core).
Axes of the slice: x: 2, y: 2, z: 4, core: 2. Of those that a mesh axis runs over, the one named last changes fastest.
Arguments:
- spectrum: float32 [36, 32, 64, 512], P('comp', None, 'space'), may hold values from 0.1 to 2
- sea_mask: int32 [64, 512], P('space'), may hold values from 0 to 1, as said below
- depth_class: int32 [64, 512], P('space'), may hold values from 0 to 3
- speed_table: float32 [4, 32], replicated, may hold values from 0.1 to 0.45
- depth_slope: float32 [2, 64, 512], P(None, 'space'), may hold values from -1 to 1
- turn_gain: float32 [32], replicated, may hold values from 0.05 to 0.3
- wind_vector: float32 [2, 64, 512], P(None, 'space'), may hold values from -4 to 4
Outputs:
- spectrum_out: float32 [36, 32, 64, 512], P('comp', None, 'space')
The draws below stay inside these ranges and needn't reach their ends.
Inputs may be any that keep to these rules, and one draw needn't show every extreme that they name: `sea_mask`: 1 marks sea and 0 land; the land share of a row grows from about 5 percent in row 0 to about 75 percent in row 63.
All inputs are finite; a program needn't handle non-finite values.
Results may differ from the reference program's by a relative error of at most 0.0003.
Values sent between devices are 32-bit elements; how exact they have to be, the bound alone decides.
A program may use at most 192 MiB of HBM per device.

```python
import math
import jax
import jax.numpy as jnp
from jax import lax

ND = 36
NF = 32
DEPTHS = 4
NX = 512
NY = 64


def draw_sea_mask(key, part):
    key = jax.random.fold_in(key, 11)
    chance = jax.random.randint(key, (NY, NX), 0, 1000)
    land_share = jnp.arange(NY) * 700 // NY + 50
    return jnp.where(chance >= land_share[:, None], 1, 0).astype(jnp.int32)


def set_ends(array, own_key, smallest, largest):
    longest = array.shape.index(max(array.shape))
    spots = []
    for shift in (0, 1):
        where = [jax.random.randint(jax.random.fold_in(own_key, axis), (), 0, length) for axis, length in enumerate(array.shape)]
        where[longest] = (where[longest] + shift) % array.shape[longest]
        spots.append(tuple(where))
    return array.at[spots[0]].set(smallest).at[spots[1]].set(largest)


def shard_levels(rng, extent, split, low, largest):
    level = 1.0
    for dim, blocks in split:
        steps = jax.random.uniform(jax.random.fold_in(jax.random.fold_in(rng, 6), dim), (blocks,), jnp.float32, low / len(split), largest / len(split))
        level = level * jnp.repeat(jnp.exp(steps), extent[dim] // blocks).reshape((-1,) + (1,) * (len(extent) - 1 - dim))
    return level


def gaussian(rng, extent, spread, bound, split=(), dtype=jnp.bfloat16):
    array = jax.random.normal(rng, extent, jnp.float32) * spread
    if len(split) > 0:
        array = shard_levels(rng, extent, split, -0.22, 0.18) * array
    return jnp.clip(array, min=-bound, max=bound).astype(dtype)


def setup_inputs(seed: int = 0) -> dict:
    key_list = jax.random.split(jax.random.key(seed), 8)
    spectrum = jnp.clip(jnp.exp(math.log(2.0) - 2.9957323 * jax.random.uniform(key_list[0], (ND, NF, NY, NX), jnp.float32) ** shard_levels(key_list[0], (ND, NF, NY, NX), ((0, 4), (2, 8)), -0.2, 0.2)), 0.1, 2.0)
    sea_mask = draw_sea_mask(jax.random.fold_in(key_list[7], 71), 0)
    depth_class = set_ends(jax.random.randint(key_list[2], (NY, NX), 0, DEPTHS), jax.random.fold_in(key_list[2], 1), 0, DEPTHS - 1).astype(jnp.int32)
    speed_table = jnp.clip(jnp.exp(jax.random.uniform(key_list[3], (DEPTHS, NF), jnp.float32, math.log(0.1), math.log(0.45))), 0.1, 0.45)
    depth_slope = jnp.clip(jax.random.uniform(key_list[4], (2, NY, NX), jnp.float32, -1.0, 1.0) * shard_levels(key_list[4], (2, NY, NX), ((1, 8),), -0.4, 0.0), -1.0, 1.0)
    turn_gain = jnp.clip(jnp.exp(jax.random.uniform(key_list[5], (NF,), jnp.float32, math.log(0.05), math.log(0.3))), 0.05, 0.3)
    wind_vector = gaussian(key_list[6], (2, NY, NX), 1.0, 4.0, ((1, 8),), jnp.float32)
    return {"spectrum": spectrum, "sea_mask": sea_mask, "depth_class": depth_class, "speed_table": speed_table, "depth_slope": depth_slope, "turn_gain": turn_gain, "wind_vector": wind_vector}


def freq_ratio(frequencies):
    position = jnp.arange(frequencies).astype(jnp.float32)
    return jnp.exp((position - 0.5 * (frequencies - 1)) * math.log(1.1))


def masked_speeds(depth_class, speed_table, wet_mask):
    speeds = jnp.zeros((speed_table.shape[1],) + depth_class.shape, jnp.float32)
    for depth_level in range(speed_table.shape[0]):
        chosen = jnp.where(depth_class == depth_level, 1.0, 0.0).astype(jnp.float32)
        speeds = speeds + chosen[None] * speed_table[depth_level][:, None, None]
    return speeds * wet_mask


def quick_flux(behind, centre, forward, beyond, courant):
    magnitude = jnp.abs(courant)
    shape_term = (1.0 - magnitude * magnitude) / 6.0
    rightward = 0.5 * (centre + forward) - 0.5 * magnitude * (forward - centre) - shape_term * (forward - 2.0 * centre + behind)
    leftward = 0.5 * (centre + forward) - 0.5 * magnitude * (centre - forward) - shape_term * (centre - 2.0 * forward + beyond)
    return courant * jnp.where(courant >= 0.0, rightward, leftward)


def advect(padded, speeds, cosine, sine_dir):
    inside = padded.shape[-2] - 4
    centre = padded[..., 2:inside + 2, :]
    middle = speeds[..., 2:inside + 2, :]
    face_along = jnp.minimum(middle, jnp.roll(middle, -1, -1)) * cosine
    flux_along = quick_flux(jnp.roll(centre, 1, -1), centre, jnp.roll(centre, -1, -1), jnp.roll(centre, -2, -1), face_along)
    face_across = jnp.minimum(speeds[..., 1:inside + 2, :], speeds[..., 2:inside + 3, :]) * sine_dir
    flux_across = quick_flux(padded[..., 0:inside + 1, :], padded[..., 1:inside + 2, :], padded[..., 2:inside + 3, :], padded[..., 3:inside + 4, :], face_across)
    return centre - (flux_along - jnp.roll(flux_along, 1, -1)) - (flux_across[..., 1:, :] - flux_across[..., :-1, :])


def refract(extended, turning):
    inside = extended.shape[0] - 4
    face_turn = 0.5 * (turning[1:inside + 2] + turning[2:inside + 3])
    flux_turn = quick_flux(extended[0:inside + 1], extended[1:inside + 2], extended[2:inside + 3], extended[3:inside + 4], face_turn)
    return extended[2:inside + 2] - (flux_turn[1:] - flux_turn[:-1])


def apply_sources(waves, energy, moment, wind_vector, wet_mask, cosine, sine_dir, freq_scale):
    mean_freq = moment / jnp.maximum(energy, 0.25)
    steepness = energy * mean_freq * mean_freq / 4.0
    projected = wind_vector[0] * cosine + wind_vector[1] * sine_dir
    growth = 0.2 * jnp.maximum(projected * freq_scale - 1.0, 0.0)
    damping = 0.25 * freq_scale * freq_scale * (steepness * steepness / jnp.maximum(mean_freq, 0.5))
    return waves * (1.0 + growth) / (1.0 + damping) * wet_mask


def reference(spectrum, sea_mask, depth_class, speed_table, depth_slope, turn_gain, wind_vector):
    all_dirs = spectrum.shape[0]
    frequencies = spectrum.shape[1]
    wet_mask = sea_mask.astype(jnp.float32)
    speeds = masked_speeds(depth_class, speed_table, wet_mask)
    angles = (jnp.arange(all_dirs).astype(jnp.float32) + 0.5) * (2.0 * math.pi / all_dirs)
    cosine = jnp.cos(angles)[:, None, None]
    sine_dir = jnp.sin(angles)[:, None, None]
    ratios = freq_ratio(frequencies)
    weights = ratios / (all_dirs * jnp.sum(ratios))

    def propagate(totals, inputs):
        waves, speed_plane, gain, weight, ratio_now = inputs
        waves = waves * wet_mask
        padded_speed = jnp.pad(speed_plane, ((2, 2), (0, 0)))
        for substep in range(2):
            padded = jnp.pad(waves, ((0, 0), (2, 2), (0, 0)))
            waves = advect(padded, padded_speed, cosine, sine_dir)
        turning = gain * (sine_dir * depth_slope[0] - cosine * depth_slope[1]) * wet_mask
        extended = jnp.concatenate([waves[-2:], waves, waves[:2]], 0)
        turn_ext = jnp.concatenate([turning[-2:], turning, turning[:2]], 0)
        waves = refract(extended, turn_ext)
        weighted = waves * weight
        totals = (totals[0] + jnp.sum(weighted, axis=0), totals[1] + jnp.sum(weighted * ratio_now, axis=0))
        return totals, waves

    zeros = jnp.zeros(spectrum.shape[2:], jnp.float32)
    sums, moved = lax.scan(propagate, (zeros, zeros), (jnp.moveaxis(spectrum, 1, 0), speeds, turn_gain, weights, ratios))
    energy, moment = sums

    def finish(inputs):
        waves, ratio_now = inputs
        return apply_sources(waves, energy, moment, wind_vector, wet_mask, cosine, sine_dir, ratio_now)

    result = lax.map(finish, (moved, ratios))
    return jnp.moveaxis(result, 0, 1)
```

```python
import functools
import math

import jax
import jax.numpy as jnp
from jax import lax
from jax.experimental import pallas as pl
from jax.experimental.pallas import tpu as pltpu
from jax.sharding import PartitionSpec as P

MESH = pl.DeviceIdType.MESH
LANES = 8


def freq_ratio(frequencies):
    position = jnp.arange(frequencies).astype(jnp.float32)
    return jnp.exp((position - 0.5 * (frequencies - 1)) * math.log(1.1))


def upwind(courant, half, third, cell, ahead, behind):
    bend = ahead + (1.0 / 3.0 + third) * (behind - ahead)
    return courant * (cell + (0.5 - half) * bend)


def scaled(speed, factor):
    return speed * factor, speed * (0.5 * factor), speed * (factor * (1.0 / 3.0))


def kernel(
    dims, cos_ref, sin_ref, fsin_ref, fcos_ref, x_ref, code_ref, slope_ref, table_ref, gain_ref,
    wgt_ref, wgtr_ref, out_ref, sums_ref, code, speed, along, across, q0, q1, q2, zlo, zhi, turn, q3,
    acc, part, peers, code_s, code_r, h0_s, h0_r, h1_s, h1_r, z_s, z_r, e_s, e_r,
):
    groups, spaces, dirs, blocks, rows, cols = dims
    depths = table_ref.shape[0]
    me = lax.axis_index("comp")
    sp = lax.axis_index("space")
    southward = (2 * me) // groups
    westward = ((4 * me // groups + 1) // 2) % 2
    sgn = 1 - 2 * southward
    first = southward * (rows - 1)
    down = sp + sgn
    up = sp - sgn
    has_down = jnp.logical_and(down >= 0, down < spaces)
    has_up = jnp.logical_and(up >= 0, up < spaces)
    right = lax.rem(me + 1, groups)
    left = lax.rem(me + groups - 1, groups)

    barrier = pltpu.get_barrier_semaphore()
    for has, other in ((has_down, down), (has_up, up)):

        @pl.when(has)
        def _():
            pl.semaphore_signal(barrier, inc=1, device_id=(me, other), device_id_type=MESH)

    for step in range(1, groups):
        pl.semaphore_signal(
            barrier, inc=1, device_id=(lax.rem(me + step, groups), sp), device_id_type=MESH
        )

    land = jnp.full((LANES, cols), -1.0, jnp.float32)
    for r in range(rows):
        code[1 + first + sgn * r] = jnp.broadcast_to(code_ref[r : r + 1, :], (LANES, cols))

    @pl.when(jnp.logical_not(has_up))
    def _():
        code[0] = land
        for b in range(blocks):
            for q in (q0, q1):
                q[b, :, 0:2] = jnp.zeros((dirs, 2, LANES, cols), jnp.float32)

    @pl.when(jnp.logical_not(has_down))
    def _():
        code[rows + 1] = land
        for b in range(blocks):
            for q in (q0, q1):
                q[b, :, rows + 2 : rows + 3] = jnp.zeros((dirs, 1, LANES, cols), jnp.float32)

    pl.semaphore_wait(barrier, groups - 1 + has_down.astype(jnp.int32) + has_up.astype(jnp.int32))

    def remote(src, dst, ssem, rsem, target):
        return pltpu.make_async_remote_copy(
            src_ref=src, dst_ref=dst, send_sem=ssem, recv_sem=rsem, device_id=target,
            device_id_type=MESH,
        )

    code_copies = (
        remote(code.at[rows], code.at[0], code_s.at[0], code_r.at[0], (me, down)),
        remote(code.at[1], code.at[rows + 1], code_s.at[1], code_r.at[1], (me, up)),
    )
    parts = ((0, 4), (4, dirs - 4))

    def halo(q, ssem, rsem, part_no, b):
        start, count = parts[part_no]
        ks = pl.ds(start, count)
        return (
            remote(
                q.at[b, ks, pl.ds(rows, 2)], q.at[b, ks, pl.ds(0, 2)],
                ssem.at[part_no, b, 0], rsem.at[part_no, b, 0], (me, down),
            ),
            remote(
                q.at[b, ks, pl.ds(2, 1)], q.at[b, ks, pl.ds(rows + 2, 1)],
                ssem.at[part_no, b, 1], rsem.at[part_no, b, 1], (me, up),
            ),
        )

    def start(copies):
        pl.when(has_down)(copies[0].start)
        pl.when(has_up)(copies[1].start)

    def wait_recv(copies):
        pl.when(has_up)(copies[0].wait_recv)
        pl.when(has_down)(copies[1].wait_recv)

    def wait_send(copies):
        pl.when(has_down)(copies[0].wait_send)
        pl.when(has_up)(copies[1].wait_send)

    start(code_copies)

    def place(p, part_no):
        return p + (p // 2) * (dirs - 4) if part_no == 0 else p - 2

    def load(part_no):
        lo, count = parts[part_no]

        def block(b, _):
            def one(p, _):
                k = place(p, part_no)
                tile = x_ref[k, pl.ds(b * LANES, LANES)]
                tile = jnp.swapaxes(tile, 0, 1)
                for r in range(rows):
                    j = first + sgn * r
                    q0[b, p, 2 + j] = jnp.where(code[1 + j] >= 0.0, tile[r], 0.0)
                return 0

            lax.fori_loop(lo, lo + count, one, 0)
            start(halo(q0, h0_s, h0_r, part_no, b))
            return 0

        lax.fori_loop(0, blocks, block, 0)

    def shifts(west):
        ahead, back = (1, cols - 1) if west else (cols - 1, 1)
        return (lambda v: pltpu.roll(v, ahead, 1)), (lambda v: pltpu.roll(v, back, 1))

    def prepare(west):
        nxt, _ = shifts(west)

        def block(b, _):
            for j in range(rows + 2):
                now = code[j]
                value = jnp.zeros((LANES, cols), jnp.float32)
                for level in range(depths):
                    value = jnp.where(now == float(level), table_ref[level, b], value)
                speed[j] = value
            for j in range(rows):
                value = speed[1 + j]
                along[b, j] = jnp.minimum(value, nxt(value))
            for j in range(rows + 1):
                across[b, j] = jnp.minimum(speed[j], speed[j + 1])
            return 0

        lax.fori_loop(0, blocks, block, 0)

    def substep(west, src, b, p, write):
        nxt, prv = shifts(west)
        cosine = cos_ref[p]
        sine = sin_ref[p]
        behind = src[b, p, 1] - src[b, p, 0]
        cell = src[b, p, 1]
        flux_in = None
        for i in range(rows + 1):
            after = src[b, p, i + 2]
            ahead = after - cell
            flux = upwind(*scaled(across[b, i], sine), cell, ahead, behind)
            if i > 0:
                step = nxt(cell) - cell
                fx = upwind(*scaled(along[b, i - 1], cosine), cell, step, prv(step))
                write(i - 1, cell - (fx - prv(fx)) - (flux - flux_in))
            flux_in = flux
            behind = ahead
            cell = after

    def first_pass(west, part_no):
        lo, count = parts[part_no]

        def block(b, _):
            wait_recv(halo(q0, h0_s, h0_r, part_no, b))

            def one(p, _):
                def write(j, value):
                    q1[b, p, 2 + j] = value

                substep(west, q0, b, p, write)
                return 0

            lax.fori_loop(lo, lo + count, one, 0)
            start(halo(q1, h1_s, h1_r, part_no, b))
            return 0

        lax.fori_loop(0, blocks, block, 0)

    def exchange(b):
        return (
            remote(
                q2.at[b, pl.ds(dirs - 2, 2)], zlo.at[b], z_s.at[b, 0], z_r.at[b, 0], (right, sp)
            ),
            remote(q2.at[b, pl.ds(0, 2)], zhi.at[b], z_s.at[b, 1], z_r.at[b, 1], (left, sp)),
        )

    def second_pass(west, part_no):
        lo, count = parts[part_no]

        def block(b, _):
            wait_recv(halo(q1, h1_s, h1_r, part_no, b))

            def one(p, _):
                k = place(p, part_no)

                def write(j, value):
                    q2[b, k, first + sgn * j] = value

                substep(west, q1, b, p, write)
                return 0

            lax.fori_loop(lo, lo + count, one, 0)
            if part_no == 0:
                for copy in exchange(b):
                    copy.start()
            return 0

        lax.fori_loop(0, blocks, block, 0)

    def both(fn):
        @pl.when(westward == 0)
        def _():
            fn(False)

        @pl.when(westward == 1)
        def _():
            fn(True)

    load(0)
    wait_recv(code_copies)

    def stage(west):
        prepare(west)
        first_pass(west, 0)
        load(1)
        second_pass(west, 0)
        first_pass(west, 1)

    both(stage)

    for face in range(dirs + 1):
        rate = fsin_ref[face] * slope_ref[0] - fcos_ref[face] * slope_ref[1]
        rate = jnp.where(code_ref[...] >= 0.0, rate, 0.0)
        for r in range(rows):
            turn[face, r] = jnp.broadcast_to(rate[r : r + 1, :], (LANES, cols))

    both(lambda west: second_pass(west, 1))

    acc[...] = jnp.zeros(acc.shape, jnp.float32)

    def refract(b, _):
        for copy in exchange(b):
            copy.wait_recv()
        gain = gain_ref[b]

        def row(r, _):
            def wave(k):
                if k < 0:
                    return zlo[b, k + 2, r]
                if k >= dirs:
                    return zhi[b, k - dirs, r]
                return q2[b, k, r]

            total = jnp.zeros((LANES, cols), jnp.float32)
            before, here, after = wave(-2), wave(-1), wave(0)
            d_left, d_mid = here - before, after - here
            flux_in = None
            for face in range(dirs + 1):
                beyond = wave(face + 1)
                d_right = beyond - after
                courant = gain * turn[face, r]
                size = jnp.abs(courant)
                positive = courant >= 0.0
                bend = d_mid + (1.0 / 3.0 + size * (1.0 / 3.0)) * (
                    jnp.where(positive, d_left, d_right) - d_mid
                )
                bend = bend * (0.5 - 0.5 * size)
                flux = courant * jnp.where(positive, here + bend, after - bend)
                if face > 0:
                    value = here - (flux - flux_in)
                    q3[face - 1, r] = value
                    total = total + value
                flux_in = flux
                here, after = after, beyond
                d_left, d_mid = d_mid, d_right
            acc[0, r] += total * wgt_ref[b]
            acc[1, r] += total * wgtr_ref[b]
            return 0

        lax.fori_loop(0, rows, row, 0)

        def put(k, _):
            out_ref[k, pl.ds(b * LANES, LANES)] = jnp.swapaxes(q3[k], 0, 1)
            return 0

        lax.fori_loop(0, dirs, put, 0)
        return 0

    lax.fori_loop(0, blocks, refract, 0)

    for m in range(2):
        part[m] = jnp.sum(acc[m], axis=1)
    sums = [
        remote(part, peers.at[step - 1], e_s.at[step - 1], e_r.at[step - 1],
               (lax.rem(me + step, groups), sp))
        for step in range(1, groups)
    ]
    for copy in sums:
        copy.start()

    wait_send(code_copies)

    def drain(b, _):
        for part_no in range(2):
            wait_send(halo(q0, h0_s, h0_r, part_no, b))
            wait_send(halo(q1, h1_s, h1_r, part_no, b))
        for copy in exchange(b):
            copy.wait_send()
        return 0

    lax.fori_loop(0, blocks, drain, 0)
    total = part[...]
    for step, copy in enumerate(sums):
        copy.wait()
        total = total + peers[step]
    sums_ref[...] = total


def local(spectrum, sea_mask, depth_class, speed_table, depth_slope, turn_gain, wind_vector):
    dirs, freqs, rows, cols = spectrum.shape
    groups = lax.axis_size("comp")
    spaces = lax.axis_size("space")
    assert groups % 4 == 0 and freqs % LANES == 0 and dirs > 4
    all_dirs = dirs * groups
    blocks = freqs // LANES
    offset = lax.axis_index("comp") * dirs
    step_angle = 2.0 * math.pi / all_dirs
    angles = ((offset + jnp.arange(dirs)).astype(jnp.float32) + 0.5) * step_angle
    cosine, sine_dir = jnp.cos(angles), jnp.sin(angles)
    places = jnp.array([0, 1, dirs - 2, dirs - 1] + list(range(2, dirs - 2)))
    ext = ((offset - 1 + jnp.arange(dirs + 2)).astype(jnp.float32) + 0.5) * step_angle
    ext_s, ext_c = jnp.sin(ext), jnp.cos(ext)
    face_s, face_c = 0.5 * (ext_s[1:] + ext_s[:-1]), 0.5 * (ext_c[1:] + ext_c[:-1])
    code = jnp.where(sea_mask > 0, depth_class, -1).astype(jnp.float32)
    ratios = freq_ratio(freqs)
    weights = ratios / (all_dirs * jnp.sum(ratios))

    def spread(v):
        shape = v.shape[:-1] + (blocks, LANES, cols)
        return jnp.broadcast_to(v.reshape(v.shape[:-1] + (blocks, LANES, 1)), shape)

    vmem = pl.BlockSpec(memory_space=pltpu.VMEM)
    smem = pl.BlockSpec(memory_space=pltpu.SMEM)
    f32 = jnp.float32
    tile = (LANES, cols)
    dma = pltpu.SemaphoreType.DMA
    waves, (energy, moment) = pl.pallas_call(
        functools.partial(kernel, (groups, spaces, dirs, blocks, rows, cols)),
        out_shape=(
            jax.ShapeDtypeStruct(spectrum.shape, f32),
            jax.ShapeDtypeStruct((2, rows, cols), f32),
        ),
        in_specs=[smem] * 4 + [vmem] * 7,
        out_specs=(vmem, vmem),
        scratch_shapes=[
            pltpu.VMEM((rows + 2,) + tile, f32),
            pltpu.VMEM((rows + 2,) + tile, f32),
            pltpu.VMEM((blocks, rows) + tile, f32),
            pltpu.VMEM((blocks, rows + 1) + tile, f32),
            pltpu.VMEM((blocks, dirs, rows + 3) + tile, f32),
            pltpu.VMEM((blocks, dirs, rows + 3) + tile, f32),
            pltpu.VMEM((blocks, dirs, rows) + tile, f32),
            pltpu.VMEM((blocks, 2, rows) + tile, f32),
            pltpu.VMEM((blocks, 2, rows) + tile, f32),
            pltpu.VMEM((dirs + 1, rows) + tile, f32),
            pltpu.VMEM((dirs, rows) + tile, f32),
            pltpu.VMEM((2, rows) + tile, f32),
            pltpu.VMEM((2, rows, cols), f32),
            pltpu.VMEM((groups - 1, 2, rows, cols), f32),
            dma((2,)), dma((2,)),
            dma((2, blocks, 2)), dma((2, blocks, 2)),
            dma((2, blocks, 2)), dma((2, blocks, 2)),
            dma((blocks, 2)), dma((blocks, 2)),
            dma((groups - 1,)), dma((groups - 1,)),
        ],
        compiler_params=pltpu.CompilerParams(
            collective_id=0, has_side_effects=True, vmem_limit_bytes=52 * 1024 * 1024
        ),
    )(
        jnp.abs(cosine[places]), jnp.abs(sine_dir[places]), face_s, face_c,
        spectrum, code, depth_slope, spread(speed_table), spread(turn_gain),
        spread(weights), spread(weights * ratios),
    )
    wet_mask = sea_mask.astype(f32)
    mean_freq = moment / jnp.maximum(energy, 0.25)
    steepness = energy * mean_freq * mean_freq / 4.0
    strength = 0.25 * steepness * steepness / jnp.maximum(mean_freq, 0.5)
    scale = ratios[None, :, None, None]
    cos4, sin4 = cosine[:, None, None, None], sine_dir[:, None, None, None]
    projected = wind_vector[0] * cos4 + wind_vector[1] * sin4
    growth = 0.2 * jnp.maximum(projected * scale - 1.0, 0.0)
    return waves * (1.0 + growth) / (1.0 + scale * scale * strength) * wet_mask


def solution(mesh):
    in_specs = (
        P("comp", None, "space", None),
        P("space", None),
        P("space", None),
        P(),
        P(None, "space", None),
        P(),
        P(None, "space", None),
    )
    out_specs = P("comp", None, "space", None)
    return jax.shard_map(local, mesh=mesh, in_specs=in_specs, out_specs=out_specs, check_vma=False)
```

```python
import functools
import math

import jax
import jax.numpy as jnp
import numpy as np
from jax import lax
from jax.experimental import pallas as pl
from jax.experimental.pallas import tpu as pltpu
from jax.sharding import PartitionSpec as P

MESH = pl.DeviceIdType.MESH
LANES = 8


def ratio_list(frequencies):
    return [math.exp((f - 0.5 * (frequencies - 1)) * math.log(1.1)) for f in range(frequencies)]


def circle(all_dirs):
    angles = (np.arange(all_dirs + 1) + 0.5) * (2.0 * math.pi / all_dirs)
    cosine, sine = np.cos(angles), np.sin(angles)
    before = angles - 2.0 * math.pi / all_dirs
    face_c, face_s = 0.5 * (cosine + np.cos(before)), 0.5 * (sine + np.sin(before))
    return np.concatenate([cosine, sine, face_c, face_s]).astype(np.float32)


def upwind(courant, half, third, cell, ahead, behind):
    bend = ahead + (1.0 / 3.0 + third) * (behind - ahead)
    return courant * (cell + (0.5 - half) * bend)


def scaled(speed, factor):
    return speed * factor, speed * (0.5 * factor), speed * (factor * (1.0 / 3.0))


def kernel(
    dims, circle_ref, x_ref, mask_ref, class_ref, slope_ref, table_ref, gain_ref, out_ref, sums_ref,
    code, lanes, speed, along, across, q0, q1, q2, zlo, zhi, turn, q3, acc, part, peers, code_s, code_r, h0_s, h0_r, h1_s, h1_r, z_s, z_r, e_s, e_r,
):
    groups, spaces, dirs, blocks, rows, cols = dims
    depths, freqs = table_ref.shape
    all_dirs = dirs * groups
    weight_sum = all_dirs * sum(ratio_list(freqs))
    me = lax.axis_index("comp")
    sp = lax.axis_index("space")
    southward = (2 * me) // groups
    westward = ((4 * me // groups + 1) // 2) % 2
    sgn = 1 - 2 * southward
    first = southward * (rows - 1)
    down = sp + sgn
    up = sp - sgn
    has_down = jnp.logical_and(down >= 0, down < spaces)
    has_up = jnp.logical_and(up >= 0, up < spaces)
    right = lax.rem(me + 1, groups)
    left = lax.rem(me + groups - 1, groups)

    barrier = pltpu.get_barrier_semaphore()
    for has, other in ((has_down, down), (has_up, up)):

        @pl.when(has)
        def _():
            pl.semaphore_signal(barrier, inc=1, device_id=(me, other), device_id_type=MESH)

    for step in range(1, groups):
        pl.semaphore_signal(
            barrier, inc=1, device_id=(lax.rem(me + step, groups), sp), device_id_type=MESH
        )

    land = jnp.full((LANES, cols), -1.0, jnp.float32)
    coded = jnp.where(mask_ref[...] > 0, class_ref[...], -1).astype(jnp.float32)
    for r in range(rows):
        code[1 + first + sgn * r] = jnp.broadcast_to(coded[r : r + 1, :], (LANES, cols))

    @pl.when(jnp.logical_not(has_up))
    def _():
        code[0] = land
        for b in range(blocks):
            for q in (q0, q1):
                q[b, :, 0:2] = jnp.zeros((dirs, 2, LANES, cols), jnp.float32)

    @pl.when(jnp.logical_not(has_down))
    def _():
        code[rows + 1] = land
        for b in range(blocks):
            for q in (q0, q1):
                q[b, :, rows + 2 : rows + 3] = jnp.zeros((dirs, 1, LANES, cols), jnp.float32)

    pl.semaphore_wait(barrier, groups - 1 + has_down.astype(jnp.int32) + has_up.astype(jnp.int32))

    def remote(src, dst, ssem, rsem, target):
        return pltpu.make_async_remote_copy(
            src_ref=src, dst_ref=dst, send_sem=ssem, recv_sem=rsem, device_id=target,
            device_id_type=MESH,
        )

    code_copies = (
        remote(code.at[rows], code.at[0], code_s.at[0], code_r.at[0], (me, down)),
        remote(code.at[1], code.at[rows + 1], code_s.at[1], code_r.at[1], (me, up)),
    )
    parts = ((0, 4), (4, dirs - 4))

    def halo(q, ssem, rsem, part_no, b):
        start, count = parts[part_no]
        ks = pl.ds(start, count)
        return (
            remote(
                q.at[b, ks, pl.ds(rows, 2)], q.at[b, ks, pl.ds(0, 2)],
                ssem.at[part_no, b, 0], rsem.at[part_no, b, 0], (me, down),
            ),
            remote(
                q.at[b, ks, pl.ds(2, 1)], q.at[b, ks, pl.ds(rows + 2, 1)],
                ssem.at[part_no, b, 1], rsem.at[part_no, b, 1], (me, up),
            ),
        )

    def start(copies):
        pl.when(has_down)(copies[0].start)
        pl.when(has_up)(copies[1].start)

    def wait_recv(copies):
        pl.when(has_up)(copies[0].wait_recv)
        pl.when(has_down)(copies[1].wait_recv)

    def wait_send(copies):
        pl.when(has_down)(copies[0].wait_send)
        pl.when(has_up)(copies[1].wait_send)

    start(code_copies)

    def place(p, part_no):
        return p + (p // 2) * (dirs - 4) if part_no == 0 else p - 2

    def load(part_no):
        lo, count = parts[part_no]

        def block(b):
            def one(p, _):
                k = place(p, part_no)
                tile = x_ref[k, pl.ds(b * LANES, LANES)]
                tile = jnp.swapaxes(tile, 0, 1)
                for r in range(rows):
                    j = first + sgn * r
                    q0[b, p, 2 + j] = jnp.where(code[1 + j] >= 0.0, tile[r], 0.0)
                return 0

            lax.fori_loop(lo, lo + count, one, 0)
            start(halo(q0, h0_s, h0_r, part_no, b))

        return block

    def shifts(west):
        ahead, back = (1, cols - 1) if west else (cols - 1, 1)
        return (lambda v: pltpu.roll(v, ahead, 1)), (lambda v: pltpu.roll(v, back, 1))

    def prepare(west):
        nxt, _ = shifts(west)
        own = lax.broadcasted_iota(jnp.int32, (freqs, freqs), 0)
        other = lax.broadcasted_iota(jnp.int32, (freqs, freqs), 1)
        for level in range(depths + 1):
            line = table_ref[level : level + 1, :] if level < depths else gain_ref[...]
            spread = jnp.where(own == other, jnp.broadcast_to(line, (freqs, freqs)), 0.0)
            column = jnp.sum(spread, axis=1, keepdims=True)
            lanes[level] = jnp.broadcast_to(column, (freqs, cols))

        def block(b, _):
            for j in range(rows + 2):
                now = code[j]
                value = jnp.zeros((LANES, cols), jnp.float32)
                for level in range(depths):
                    value = jnp.where(now == float(level), lanes[level, pl.ds(b * LANES, LANES)], value)
                speed[j] = value
            for j in range(rows):
                value = speed[1 + j]
                along[b, j] = jnp.minimum(value, nxt(value))
            for j in range(rows + 1):
                across[b, j] = jnp.minimum(speed[j], speed[j + 1])
            return 0

        lax.fori_loop(0, blocks, block, 0)

    def substep(west, src, b, p, k, write):
        nxt, prv = shifts(west)
        cosine = jnp.abs(circle_ref[me * dirs + k])
        sine = jnp.abs(circle_ref[all_dirs + 1 + me * dirs + k])
        behind = src[b, p, 1] - src[b, p, 0]
        cell = src[b, p, 1]
        flux_in = None
        for i in range(rows + 1):
            after = src[b, p, i + 2]
            ahead = after - cell
            flux = upwind(*scaled(across[b, i], sine), cell, ahead, behind)
            if i > 0:
                step = nxt(cell) - cell
                fx = upwind(*scaled(along[b, i - 1], cosine), cell, step, prv(step))
                write(i - 1, cell - (fx - prv(fx)) - (flux - flux_in))
            flux_in = flux
            behind = ahead
            cell = after

    def first_pass(west, part_no):
        lo, count = parts[part_no]

        def block(b):
            wait_recv(halo(q0, h0_s, h0_r, part_no, b))

            def one(p, _):
                def write(j, value):
                    q1[b, p, 2 + j] = value

                substep(west, q0, b, p, place(p, part_no), write)
                return 0

            lax.fori_loop(lo, lo + count, one, 0)
            start(halo(q1, h1_s, h1_r, part_no, b))

        return block

    def exchange(b):
        return (
            remote(
                q2.at[b, pl.ds(dirs - 2, 2)], zlo.at[b], z_s.at[b, 0], z_r.at[b, 0], (right, sp)
            ),
            remote(q2.at[b, pl.ds(0, 2)], zhi.at[b], z_s.at[b, 1], z_r.at[b, 1], (left, sp)),
        )

    def second_pass(west, part_no):
        lo, count = parts[part_no]

        def block(b):
            wait_recv(halo(q1, h1_s, h1_r, part_no, b))

            def one(p, _):
                k = place(p, part_no)

                def write(j, value):
                    q2[b, k, first + sgn * j] = value

                substep(west, q1, b, p, k, write)
                return 0

            lax.fori_loop(lo, lo + count, one, 0)
            if part_no == 0:
                for copy in exchange(b):
                    copy.start()

        return block

    def both(fn):
        @pl.when(westward == 0)
        def _():
            fn(False)

        @pl.when(westward == 1)
        def _():
            fn(True)

    load(0)(0)
    wait_recv(code_copies)

    def stage(west):
        prepare(west)
        jobs = ((1, load(0)), (0, first_pass(west, 0)), (0, load(1)), (-1, second_pass(west, 0)))

        def step(s, _):
            for lag, job in jobs:

                @pl.when(jnp.logical_and(s + lag >= 0, s + lag < blocks))
                def _():
                    job(s + lag)

            return 0

        lax.fori_loop(0, blocks + 1, step, 0)

        def inner(s, _):
            pl.when(s < blocks)(lambda: first_pass(west, 1)(s))
            pl.when(s > 0)(lambda: second_pass(west, 1)(s - 1))
            return 0

        lax.fori_loop(0, blocks + 1, inner, 0)

    for face in range(dirs + 1):
        face_c = circle_ref[2 * (all_dirs + 1) + me * dirs + face]
        face_s = circle_ref[3 * (all_dirs + 1) + me * dirs + face]
        rate = face_s * slope_ref[0] - face_c * slope_ref[1]
        rate = jnp.where(mask_ref[...] > 0, rate, 0.0)
        for r in range(rows):
            turn[face, r] = jnp.broadcast_to(rate[r : r + 1, :], (LANES, cols))

    both(stage)

    acc[...] = jnp.zeros(acc.shape, jnp.float32)

    def refract(b, _):
        for copy in exchange(b):
            copy.wait_recv()
        gain = lanes[depths, pl.ds(b * LANES, LANES)]
        place_f = b * LANES + lax.broadcasted_iota(jnp.int32, (LANES, cols), 0)
        ratio = jnp.exp((place_f.astype(jnp.float32) - 0.5 * (freqs - 1)) * math.log(1.1))
        weight = ratio * (1.0 / weight_sum)

        def row(r, _):
            def wave(k):
                if k < 0:
                    return zlo[b, k + 2, r]
                if k >= dirs:
                    return zhi[b, k - dirs, r]
                return q2[b, k, r]

            total = jnp.zeros((LANES, cols), jnp.float32)
            before, here, after = wave(-2), wave(-1), wave(0)
            d_left, d_mid = here - before, after - here
            flux_in = None
            for face in range(dirs + 1):
                beyond = wave(face + 1)
                d_right = beyond - after
                courant = gain * turn[face, r]
                size = jnp.abs(courant)
                positive = courant >= 0.0
                bend = d_mid + (1.0 / 3.0 + size * (1.0 / 3.0)) * (
                    jnp.where(positive, d_left, d_right) - d_mid
                )
                bend = bend * (0.5 - 0.5 * size)
                flux = courant * jnp.where(positive, here + bend, after - bend)
                if face > 0:
                    value = here - (flux - flux_in)
                    q3[face - 1, r] = value
                    total = total + value
                flux_in = flux
                here, after = after, beyond
                d_left, d_mid = d_mid, d_right
            total = total * weight
            acc[0, r] += total
            acc[1, r] += total * ratio
            return 0

        lax.fori_loop(0, rows, row, 0)

        def put(k, _):
            out_ref[k, pl.ds(b * LANES, LANES)] = jnp.swapaxes(q3[k], 0, 1)
            return 0

        lax.fori_loop(0, dirs, put, 0)
        return 0

    lax.fori_loop(0, blocks, refract, 0)

    for m in range(2):
        part[m] = jnp.sum(acc[m], axis=1)
    sums = [
        remote(part, peers.at[step - 1], e_s.at[step - 1], e_r.at[step - 1],
               (lax.rem(me + step, groups), sp))
        for step in range(1, groups)
    ]
    for copy in sums:
        copy.start()

    wait_send(code_copies)

    def drain(b, _):
        for part_no in range(2):
            wait_send(halo(q0, h0_s, h0_r, part_no, b))
            wait_send(halo(q1, h1_s, h1_r, part_no, b))
        for copy in exchange(b):
            copy.wait_send()
        return 0

    lax.fori_loop(0, blocks, drain, 0)
    total = part[...]
    for step, copy in enumerate(sums):
        copy.wait()
        total = total + peers[step]
    sums_ref[...] = total


def sources(dims, circle_ref, q_ref, sums_ref, wind_ref, mask_ref, out_ref, factor):
    dirs, all_dirs, freqs = dims
    ratios = ratio_list(freqs)
    k = pl.program_id(0)

    @pl.when(k == 0)
    def _():
        energy, moment = sums_ref[0], sums_ref[1]
        mean_freq = moment / jnp.maximum(energy, 0.25)
        steepness = energy * mean_freq * mean_freq / 4.0
        strength = 0.25 * (steepness * steepness / jnp.maximum(mean_freq, 0.5))
        wet = mask_ref[...].astype(jnp.float32)
        for f in range(freqs):
            factor[f] = wet / (1.0 + (ratios[f] * ratios[f]) * strength)

    at = lax.axis_index("comp") * dirs + k
    projected = wind_ref[0] * circle_ref[at] + wind_ref[1] * circle_ref[all_dirs + 1 + at]
    for f in range(freqs):
        growth = 0.2 * jnp.maximum(projected * ratios[f] - 1.0, 0.0)
        out_ref[0, f] = q_ref[0, f] * (1.0 + growth) * factor[f]


def local(spectrum, sea_mask, depth_class, speed_table, depth_slope, turn_gain, wind_vector):
    dirs, freqs, rows, cols = spectrum.shape
    groups = lax.axis_size("comp")
    spaces = lax.axis_size("space")
    assert groups % 4 == 0 and freqs % LANES == 0 and dirs > 4
    all_dirs = dirs * groups
    blocks = freqs // LANES
    angles = jnp.asarray(circle(all_dirs))
    vmem = pl.BlockSpec(memory_space=pltpu.VMEM)
    smem = pl.BlockSpec(memory_space=pltpu.SMEM)
    f32 = jnp.float32
    tile = (LANES, cols)
    dma = pltpu.SemaphoreType.DMA
    waves, sums = pl.pallas_call(
        functools.partial(kernel, (groups, spaces, dirs, blocks, rows, cols)),
        out_shape=(
            jax.ShapeDtypeStruct(spectrum.shape, f32),
            jax.ShapeDtypeStruct((2, rows, cols), f32),
        ),
        in_specs=[smem] + [vmem] * 6,
        out_specs=(vmem, vmem),
        scratch_shapes=[
            pltpu.VMEM((rows + 2,) + tile, f32),
            pltpu.VMEM((speed_table.shape[0] + 1, freqs, cols), f32),
            pltpu.VMEM((rows + 2,) + tile, f32),
            pltpu.VMEM((blocks, rows) + tile, f32),
            pltpu.VMEM((blocks, rows + 1) + tile, f32),
            pltpu.VMEM((blocks, dirs, rows + 3) + tile, f32),
            pltpu.VMEM((blocks, dirs, rows + 3) + tile, f32),
            pltpu.VMEM((blocks, dirs, rows) + tile, f32),
            pltpu.VMEM((blocks, 2, rows) + tile, f32),
            pltpu.VMEM((blocks, 2, rows) + tile, f32),
            pltpu.VMEM((dirs + 1, rows) + tile, f32),
            pltpu.VMEM((dirs, rows) + tile, f32),
            pltpu.VMEM((2, rows) + tile, f32),
            pltpu.VMEM((2, rows, cols), f32),
            pltpu.VMEM((groups - 1, 2, rows, cols), f32),
            dma((2,)), dma((2,)),
            dma((2, blocks, 2)), dma((2, blocks, 2)),
            dma((2, blocks, 2)), dma((2, blocks, 2)),
            dma((blocks, 2)), dma((blocks, 2)),
            dma((groups - 1,)), dma((groups - 1,)),
        ],
        compiler_params=pltpu.CompilerParams(
            collective_id=0, has_side_effects=True, vmem_limit_bytes=52 * 1024 * 1024
        ),
    )(
        angles, spectrum, sea_mask, depth_class, depth_slope, speed_table,
        turn_gain.reshape(1, freqs),
    )

    def whole(shape):
        return pl.BlockSpec(shape, lambda k: (0,) * len(shape))

    plane = pl.BlockSpec((1, freqs, rows, cols), lambda k: (k, 0, 0, 0))
    return pl.pallas_call(
        functools.partial(sources, (dirs, all_dirs, freqs)),
        grid=(dirs,),
        out_shape=jax.ShapeDtypeStruct(spectrum.shape, f32),
        in_specs=[
            smem, plane, whole((2, rows, cols)), whole((2, rows, cols)), whole((rows, cols)),
        ],
        out_specs=plane,
        scratch_shapes=[pltpu.VMEM((freqs, rows, cols), f32)],
        compiler_params=pltpu.CompilerParams(vmem_limit_bytes=24 * 1024 * 1024),
    )(angles, waves, sums, wind_vector, sea_mask)


def solution(mesh):
    in_specs = (
        P("comp", None, "space", None),
        P("space", None),
        P("space", None),
        P(),
        P(None, "space", None),
        P(),
        P(None, "space", None),
    )
    out_specs = P("comp", None, "space", None)
    return jax.shard_map(local, mesh=mesh, in_specs=in_specs, out_specs=out_specs, check_vma=False)
```

```python
import functools
import math

import jax
import jax.numpy as jnp
import numpy as np
from jax import lax
from jax.experimental import pallas as pl
from jax.experimental.pallas import tpu as pltpu
from jax.sharding import PartitionSpec as P

MESH = pl.DeviceIdType.MESH
LANES = 8


def ratio_list(frequencies):
    return [math.exp((f - 0.5 * (frequencies - 1)) * math.log(1.1)) for f in range(frequencies)]


def circle(all_dirs):
    angles = (np.arange(all_dirs + 1) + 0.5) * (2.0 * math.pi / all_dirs)
    cosine, sine = np.cos(angles), np.sin(angles)
    before = angles - 2.0 * math.pi / all_dirs
    face_c, face_s = 0.5 * (cosine + np.cos(before)), 0.5 * (sine + np.sin(before))
    return np.concatenate([cosine, sine, face_c, face_s]).astype(np.float32)


def upwind(courant, half, third, cell, ahead, behind):
    bend = ahead + (1.0 / 3.0 + third) * (behind - ahead)
    return courant * (cell + (0.5 - half) * bend)


def scaled(speed, factor):
    return speed * factor, speed * (0.5 * factor), speed * (factor * (1.0 / 3.0))


def kernel(
    dims, circle_ref, x_hbm, mask_hbm, class_hbm, slope_hbm, table_hbm, gain_hbm, out_hbm, sums_ref,
    x_ref, mask_ref, class_ref, slope_ref, table_ref, gain_ref, out_ref, in_s, x_s, out_s,
    code, lanes, speed, along, across, q0, q1, q2, zlo, zhi, turn, q3, acc, part, peers, code_s, code_r, h0_s, h0_r, h1_s, h1_r, z_s, z_r, e_s, e_r,
):
    groups, spaces, dirs, blocks, rows, cols = dims
    depths, freqs = table_ref.shape
    all_dirs = dirs * groups
    weight_sum = all_dirs * sum(ratio_list(freqs))
    me = lax.axis_index("comp")
    sp = lax.axis_index("space")
    southward = (2 * me) // groups
    westward = ((4 * me // groups + 1) // 2) % 2
    sgn = 1 - 2 * southward
    first = southward * (rows - 1)
    down = sp + sgn
    up = sp - sgn
    has_down = jnp.logical_and(down >= 0, down < spaces)
    has_up = jnp.logical_and(up >= 0, up < spaces)
    right = lax.rem(me + 1, groups)
    left = lax.rem(me + groups - 1, groups)

    barrier = pltpu.get_barrier_semaphore()
    for has, other in ((has_down, down), (has_up, up)):

        @pl.when(has)
        def _():
            pl.semaphore_signal(barrier, inc=1, device_id=(me, other), device_id_type=MESH)

    for step in range(1, groups):
        pl.semaphore_signal(
            barrier, inc=1, device_id=(lax.rem(me + step, groups), sp), device_id_type=MESH
        )

    small = [
        pltpu.make_async_copy(src, dst, in_s.at[i])
        for i, (src, dst) in enumerate(
            (
                (mask_hbm, mask_ref), (class_hbm, class_ref), (table_hbm, table_ref),
                (gain_hbm, gain_ref), (slope_hbm, slope_ref),
            )
        )
    ]
    ranges = (((0, 2), (dirs - 2, 2)), ((2, dirs - 4),))

    def fetch(part_no, b):
        return [
            pltpu.make_async_copy(
                x_hbm.at[pl.ds(k, n), pl.ds(b * LANES, LANES)], x_ref.at[b, pl.ds(k, n)],
                x_s.at[2 * part_no + i, b],
            )
            for i, (k, n) in enumerate(ranges[part_no])
        ]

    def deliver(b):
        return pltpu.make_async_copy(
            out_ref.at[b], out_hbm.at[:, pl.ds(b * LANES, LANES)], out_s.at[b]
        )

    for copy in small:
        copy.start()
    for part_no in range(2):
        for b in range(blocks):
            for copy in fetch(part_no, b):
                copy.start()
    for copy in small:
        copy.wait()

    land = jnp.full((LANES, cols), -1.0, jnp.float32)
    coded = jnp.where(mask_ref[...] > 0, class_ref[...], -1).astype(jnp.float32)
    for r in range(rows):
        code[1 + first + sgn * r] = jnp.broadcast_to(coded[r : r + 1, :], (LANES, cols))

    @pl.when(jnp.logical_not(has_up))
    def _():
        code[0] = land
        for b in range(blocks):
            for q in (q0, q1):
                q[b, :, 0:2] = jnp.zeros((dirs, 2, LANES, cols), jnp.float32)

    @pl.when(jnp.logical_not(has_down))
    def _():
        code[rows + 1] = land
        for b in range(blocks):
            for q in (q0, q1):
                q[b, :, rows + 2 : rows + 3] = jnp.zeros((dirs, 1, LANES, cols), jnp.float32)

    pl.semaphore_wait(barrier, groups - 1 + has_down.astype(jnp.int32) + has_up.astype(jnp.int32))

    def remote(src, dst, ssem, rsem, target):
        return pltpu.make_async_remote_copy(
            src_ref=src, dst_ref=dst, send_sem=ssem, recv_sem=rsem, device_id=target,
            device_id_type=MESH,
        )

    code_copies = (
        remote(code.at[rows], code.at[0], code_s.at[0], code_r.at[0], (me, down)),
        remote(code.at[1], code.at[rows + 1], code_s.at[1], code_r.at[1], (me, up)),
    )
    parts = ((0, 4), (4, dirs - 4))

    def halo(q, ssem, rsem, part_no, b):
        start, count = parts[part_no]
        ks = pl.ds(start, count)
        return (
            remote(
                q.at[b, ks, pl.ds(rows, 2)], q.at[b, ks, pl.ds(0, 2)],
                ssem.at[part_no, b, 0], rsem.at[part_no, b, 0], (me, down),
            ),
            remote(
                q.at[b, ks, pl.ds(2, 1)], q.at[b, ks, pl.ds(rows + 2, 1)],
                ssem.at[part_no, b, 1], rsem.at[part_no, b, 1], (me, up),
            ),
        )

    def start(copies):
        pl.when(has_down)(copies[0].start)
        pl.when(has_up)(copies[1].start)

    def wait_recv(copies):
        pl.when(has_up)(copies[0].wait_recv)
        pl.when(has_down)(copies[1].wait_recv)

    def wait_send(copies):
        pl.when(has_down)(copies[0].wait_send)
        pl.when(has_up)(copies[1].wait_send)

    start(code_copies)

    def place(p, part_no):
        return p + (p // 2) * (dirs - 4) if part_no == 0 else p - 2

    def load(part_no):
        lo, count = parts[part_no]

        def block(b):
            for copy in fetch(part_no, b):
                copy.wait()

            def one(p, _):
                k = place(p, part_no)
                tile = x_ref[b, k]
                tile = jnp.swapaxes(tile, 0, 1)
                for r in range(rows):
                    j = first + sgn * r
                    q0[b, p, 2 + j] = jnp.where(code[1 + j] >= 0.0, tile[r], 0.0)
                return 0

            lax.fori_loop(lo, lo + count, one, 0)
            start(halo(q0, h0_s, h0_r, part_no, b))

        return block

    def shifts(west):
        ahead, back = (1, cols - 1) if west else (cols - 1, 1)
        return (lambda v: pltpu.roll(v, ahead, 1)), (lambda v: pltpu.roll(v, back, 1))

    def prepare(west):
        nxt, _ = shifts(west)
        own = lax.broadcasted_iota(jnp.int32, (freqs, freqs), 0)
        other = lax.broadcasted_iota(jnp.int32, (freqs, freqs), 1)
        for level in range(depths + 1):
            line = table_ref[level : level + 1, :] if level < depths else gain_ref[...]
            spread = jnp.where(own == other, jnp.broadcast_to(line, (freqs, freqs)), 0.0)
            column = jnp.sum(spread, axis=1, keepdims=True)
            lanes[level] = jnp.broadcast_to(column, (freqs, cols))

        def block(b, _):
            for j in range(rows + 2):
                now = code[j]
                value = jnp.zeros((LANES, cols), jnp.float32)
                for level in range(depths):
                    value = jnp.where(now == float(level), lanes[level, pl.ds(b * LANES, LANES)], value)
                speed[j] = value
            for j in range(rows):
                value = speed[1 + j]
                along[b, j] = jnp.minimum(value, nxt(value))
            for j in range(rows + 1):
                across[b, j] = jnp.minimum(speed[j], speed[j + 1])
            return 0

        lax.fori_loop(0, blocks, block, 0)

    def substep(west, src, b, p, k, write):
        nxt, prv = shifts(west)
        cosine = jnp.abs(circle_ref[me * dirs + k])
        sine = jnp.abs(circle_ref[all_dirs + 1 + me * dirs + k])
        behind = src[b, p, 1] - src[b, p, 0]
        cell = src[b, p, 1]
        flux_in = None
        for i in range(rows + 1):
            after = src[b, p, i + 2]
            ahead = after - cell
            flux = upwind(*scaled(across[b, i], sine), cell, ahead, behind)
            if i > 0:
                step = nxt(cell) - cell
                fx = upwind(*scaled(along[b, i - 1], cosine), cell, step, prv(step))
                write(i - 1, cell - (fx - prv(fx)) - (flux - flux_in))
            flux_in = flux
            behind = ahead
            cell = after

    def first_pass(west, part_no):
        lo, count = parts[part_no]

        def block(b):
            wait_recv(halo(q0, h0_s, h0_r, part_no, b))

            def one(p, _):
                def write(j, value):
                    q1[b, p, 2 + j] = value

                substep(west, q0, b, p, place(p, part_no), write)
                return 0

            lax.fori_loop(lo, lo + count, one, 0)
            start(halo(q1, h1_s, h1_r, part_no, b))

        return block

    half = rows // 2

    def exchange(b, h):
        at = pl.ds(h * half, half)
        return (
            remote(
                q2.at[b, pl.ds(dirs - 2, 2), at], zlo.at[b, :, at],
                z_s.at[b, h, 0], z_r.at[b, h, 0], (right, sp),
            ),
            remote(
                q2.at[b, pl.ds(0, 2), at], zhi.at[b, :, at],
                z_s.at[b, h, 1], z_r.at[b, h, 1], (left, sp),
            ),
        )

    def second_pass(west, part_no):
        lo, count = parts[part_no]

        def block(b):
            wait_recv(halo(q1, h1_s, h1_r, part_no, b))

            def one(p, _):
                k = place(p, part_no)

                def write(j, value):
                    q2[b, k, first + sgn * j] = value

                substep(west, q1, b, p, k, write)
                return 0

            lax.fori_loop(lo, lo + count, one, 0)
            if part_no == 0:
                for h in range(2):
                    for copy in exchange(b, h):
                        copy.start()

        return block

    def both(fn):
        @pl.when(westward == 0)
        def _():
            fn(False)

        @pl.when(westward == 1)
        def _():
            fn(True)

    load(0)(0)
    wait_recv(code_copies)

    def stage(west):
        prepare(west)
        jobs = ((1, load(0)), (0, first_pass(west, 0)), (0, load(1)), (-1, second_pass(west, 0)))

        def step(s, _):
            for lag, job in jobs:

                @pl.when(jnp.logical_and(s + lag >= 0, s + lag < blocks))
                def _():
                    job(s + lag)

            return 0

        lax.fori_loop(0, blocks + 1, step, 0)

        def inner(s, _):
            pl.when(s < blocks)(lambda: first_pass(west, 1)(s))
            pl.when(s > 0)(lambda: second_pass(west, 1)(s - 1))
            return 0

        lax.fori_loop(0, blocks + 1, inner, 0)

    for face in range(dirs + 1):
        face_c = circle_ref[2 * (all_dirs + 1) + me * dirs + face]
        face_s = circle_ref[3 * (all_dirs + 1) + me * dirs + face]
        rate = face_s * slope_ref[0] - face_c * slope_ref[1]
        rate = jnp.where(mask_ref[...] > 0, rate, 0.0)
        for r in range(rows):
            turn[face, r] = jnp.broadcast_to(rate[r : r + 1, :], (LANES, cols))

    both(stage)

    acc[...] = jnp.zeros(acc.shape, jnp.float32)

    def refract(b, _):
        gain = lanes[depths, pl.ds(b * LANES, LANES)]
        place_f = b * LANES + lax.broadcasted_iota(jnp.int32, (LANES, cols), 0)
        ratio = jnp.exp((place_f.astype(jnp.float32) - 0.5 * (freqs - 1)) * math.log(1.1))
        weight = ratio * (1.0 / weight_sum)

        def row(r, _):
            def wave(k):
                if k < 0:
                    return zlo[b, k + 2, r]
                if k >= dirs:
                    return zhi[b, k - dirs, r]
                return q2[b, k, r]

            total = jnp.zeros((LANES, cols), jnp.float32)
            before, here, after = wave(-2), wave(-1), wave(0)
            d_left, d_mid = here - before, after - here
            flux_in = None
            for face in range(dirs + 1):
                beyond = wave(face + 1)
                d_right = beyond - after
                courant = gain * turn[face, r]
                size = jnp.abs(courant)
                positive = courant >= 0.0
                bend = d_mid + (1.0 / 3.0 + size * (1.0 / 3.0)) * (
                    jnp.where(positive, d_left, d_right) - d_mid
                )
                bend = bend * (0.5 - 0.5 * size)
                flux = courant * jnp.where(positive, here + bend, after - bend)
                if face > 0:
                    value = here - (flux - flux_in)
                    q3[face - 1, r] = value
                    total = total + value
                flux_in = flux
                here, after = after, beyond
                d_left, d_mid = d_mid, d_right
            total = total * weight
            acc[0, r] += total
            acc[1, r] += total * ratio
            return 0

        def piece(h, _):
            for copy in exchange(b, h):
                copy.wait_recv()
            lax.fori_loop(h * half, (h + 1) * half, row, 0)
            return 0

        lax.fori_loop(0, 2, piece, 0)

        def put(k, _):
            out_ref[b, k] = jnp.swapaxes(q3[k], 0, 1)
            return 0

        lax.fori_loop(0, dirs, put, 0)
        deliver(b).start()
        return 0

    lax.fori_loop(0, blocks, refract, 0)

    for m in range(2):
        part[m] = jnp.sum(acc[m], axis=1)
    sums = [
        remote(part, peers.at[step - 1], e_s.at[step - 1], e_r.at[step - 1],
               (lax.rem(me + step, groups), sp))
        for step in range(1, groups)
    ]
    for copy in sums:
        copy.start()

    wait_send(code_copies)

    def drain(b, _):
        for part_no in range(2):
            wait_send(halo(q0, h0_s, h0_r, part_no, b))
            wait_send(halo(q1, h1_s, h1_r, part_no, b))
        for h in range(2):
            for copy in exchange(b, h):
                copy.wait_send()
        deliver(b).wait()
        return 0

    lax.fori_loop(0, blocks, drain, 0)
    total = part[...]
    for step, copy in enumerate(sums):
        copy.wait()
        total = total + peers[step]
    sums_ref[...] = total


def sources(dims, circle_ref, q_ref, sums_ref, wind_ref, mask_ref, out_ref, factor):
    dirs, all_dirs, freqs = dims
    ratios = ratio_list(freqs)
    k = pl.program_id(0)

    @pl.when(k == 0)
    def _():
        energy, moment = sums_ref[0], sums_ref[1]
        mean_freq = moment / jnp.maximum(energy, 0.25)
        steepness = energy * mean_freq * mean_freq / 4.0
        strength = 0.25 * (steepness * steepness / jnp.maximum(mean_freq, 0.5))
        wet = mask_ref[...].astype(jnp.float32)
        for f in range(freqs):
            factor[f] = wet / (1.0 + (ratios[f] * ratios[f]) * strength)

    at = lax.axis_index("comp") * dirs + k
    projected = wind_ref[0] * circle_ref[at] + wind_ref[1] * circle_ref[all_dirs + 1 + at]
    for f in range(freqs):
        growth = 0.2 * jnp.maximum(projected * ratios[f] - 1.0, 0.0)
        out_ref[0, f] = q_ref[0, f] * (1.0 + growth) * factor[f]


def local(spectrum, sea_mask, depth_class, speed_table, depth_slope, turn_gain, wind_vector):
    dirs, freqs, rows, cols = spectrum.shape
    groups = lax.axis_size("comp")
    spaces = lax.axis_size("space")
    assert groups % 4 == 0 and freqs % LANES == 0 and dirs > 4 and rows % 2 == 0
    all_dirs = dirs * groups
    blocks = freqs // LANES
    angles = jnp.asarray(circle(all_dirs))
    vmem = pl.BlockSpec(memory_space=pltpu.VMEM)
    smem = pl.BlockSpec(memory_space=pltpu.SMEM)
    hbm = pl.BlockSpec(memory_space=pl.ANY)
    f32 = jnp.float32
    tile = (LANES, cols)
    dma = pltpu.SemaphoreType.DMA
    waves, sums = pl.pallas_call(
        functools.partial(kernel, (groups, spaces, dirs, blocks, rows, cols)),
        out_shape=(
            jax.ShapeDtypeStruct(spectrum.shape, f32),
            jax.ShapeDtypeStruct((2, rows, cols), f32),
        ),
        in_specs=[smem] + [hbm] * 6,
        out_specs=(hbm, vmem),
        scratch_shapes=[
            pltpu.VMEM((blocks, dirs, LANES, rows, cols), f32),
            pltpu.VMEM((rows, cols), jnp.int32),
            pltpu.VMEM((rows, cols), jnp.int32),
            pltpu.VMEM((2, rows, cols), f32),
            pltpu.VMEM(speed_table.shape, f32),
            pltpu.VMEM((1, freqs), f32),
            pltpu.VMEM((blocks, dirs, LANES, rows, cols), f32),
            dma((5,)), dma((3, blocks)), dma((blocks,)),
            pltpu.VMEM((rows + 2,) + tile, f32),
            pltpu.VMEM((speed_table.shape[0] + 1, freqs, cols), f32),
            pltpu.VMEM((rows + 2,) + tile, f32),
            pltpu.VMEM((blocks, rows) + tile, f32),
            pltpu.VMEM((blocks, rows + 1) + tile, f32),
            pltpu.VMEM((blocks, dirs, rows + 3) + tile, f32),
            pltpu.VMEM((blocks, dirs, rows + 3) + tile, f32),
            pltpu.VMEM((blocks, dirs, rows) + tile, f32),
            pltpu.VMEM((blocks, 2, rows) + tile, f32),
            pltpu.VMEM((blocks, 2, rows) + tile, f32),
            pltpu.VMEM((dirs + 1, rows) + tile, f32),
            pltpu.VMEM((dirs, rows) + tile, f32),
            pltpu.VMEM((2, rows) + tile, f32),
            pltpu.VMEM((2, rows, cols), f32),
            pltpu.VMEM((groups - 1, 2, rows, cols), f32),
            dma((2,)), dma((2,)),
            dma((2, blocks, 2)), dma((2, blocks, 2)),
            dma((2, blocks, 2)), dma((2, blocks, 2)),
            dma((blocks, 2, 2)), dma((blocks, 2, 2)),
            dma((groups - 1,)), dma((groups - 1,)),
        ],
        compiler_params=pltpu.CompilerParams(
            collective_id=0, has_side_effects=True, vmem_limit_bytes=60 * 1024 * 1024
        ),
    )(
        angles, spectrum, sea_mask, depth_class, depth_slope, speed_table,
        turn_gain.reshape(1, freqs),
    )

    def whole(shape):
        return pl.BlockSpec(shape, lambda k: (0,) * len(shape))

    plane = pl.BlockSpec((1, freqs, rows, cols), lambda k: (k, 0, 0, 0))
    return pl.pallas_call(
        functools.partial(sources, (dirs, all_dirs, freqs)),
        grid=(dirs,),
        out_shape=jax.ShapeDtypeStruct(spectrum.shape, f32),
        in_specs=[
            smem, plane, whole((2, rows, cols)), whole((2, rows, cols)), whole((rows, cols)),
        ],
        out_specs=plane,
        scratch_shapes=[pltpu.VMEM((freqs, rows, cols), f32)],
        compiler_params=pltpu.CompilerParams(vmem_limit_bytes=60 * 1024 * 1024),
    )(angles, waves, sums, wind_vector, sea_mask)


def solution(mesh):
    in_specs = (
        P("comp", None, "space", None),
        P("space", None),
        P("space", None),
        P(),
        P(None, "space", None),
        P(),
        P(None, "space", None),
    )
    out_specs = P("comp", None, "space", None)
    return jax.shard_map(local, mesh=mesh, in_specs=in_specs, out_specs=out_specs, check_vma=False)
```

```python
import functools
import math

import jax
import jax.numpy as jnp
import numpy as np
from jax import lax
from jax.experimental import pallas as pl
from jax.experimental.pallas import tpu as pltpu
from jax.sharding import PartitionSpec as P

MESH = pl.DeviceIdType.MESH
LANES = 8


def ratio_list(frequencies):
    return [math.exp((f - 0.5 * (frequencies - 1)) * math.log(1.1)) for f in range(frequencies)]


def circle(all_dirs):
    angles = (np.arange(all_dirs + 1) + 0.5) * (2.0 * math.pi / all_dirs)
    cosine, sine = np.cos(angles), np.sin(angles)
    before = angles - 2.0 * math.pi / all_dirs
    face_c, face_s = 0.5 * (cosine + np.cos(before)), 0.5 * (sine + np.sin(before))
    return np.concatenate([cosine, sine, face_c, face_s]).astype(np.float32)


def upwind(courant, half, third, cell, ahead, behind):
    bend = ahead + (1.0 / 3.0 + third) * (behind - ahead)
    return courant * (cell + (0.5 - half) * bend)


def scaled(speed, factor):
    return speed * factor, speed * (0.5 * factor), speed * (factor * (1.0 / 3.0))


def kernel(
    dims, circle_ref, x_hbm, mask_hbm, class_hbm, slope_hbm, table_hbm, gain_hbm, out_hbm, sums_ref,
    x_ref, mask_ref, class_ref, slope_ref, table_ref, gain_ref, out_ref, in_s, x_s, out_s,
    code, lanes, speed, along, across, q0, q1, q2, zlo, zhi, turn, q3, acc, part, peers, code_s, code_r, h0_s, h0_r, h1_s, h1_r, z_s, z_r, e_s, e_r,
):
    groups, spaces, dirs, blocks, rows, cols = dims
    depths, freqs = table_ref.shape
    all_dirs = dirs * groups
    weight_sum = all_dirs * sum(ratio_list(freqs))
    me = lax.axis_index("comp")
    sp = lax.axis_index("space")
    southward = (2 * me) // groups
    westward = ((4 * me // groups + 1) // 2) % 2
    sgn = 1 - 2 * southward
    first = southward * (rows - 1)
    down = sp + sgn
    up = sp - sgn
    has_down = jnp.logical_and(down >= 0, down < spaces)
    has_up = jnp.logical_and(up >= 0, up < spaces)
    right = lax.rem(me + 1, groups)
    left = lax.rem(me + groups - 1, groups)

    barrier = pltpu.get_barrier_semaphore()
    for has, other in ((has_down, down), (has_up, up)):

        @pl.when(has)
        def _():
            pl.semaphore_signal(barrier, inc=1, device_id=(me, other), device_id_type=MESH)

    for step in range(1, groups):
        pl.semaphore_signal(
            barrier, inc=1, device_id=(lax.rem(me + step, groups), sp), device_id_type=MESH
        )

    small = [
        pltpu.make_async_copy(src, dst, in_s.at[i])
        for i, (src, dst) in enumerate(
            (
                (mask_hbm, mask_ref), (class_hbm, class_ref), (table_hbm, table_ref),
                (gain_hbm, gain_ref), (slope_hbm, slope_ref),
            )
        )
    ]
    ranges = (((0, 2), (dirs - 2, 2)), ((2, dirs - 4),))

    def fetch(part_no, b):
        return [
            pltpu.make_async_copy(
                x_hbm.at[pl.ds(k, n), pl.ds(b * LANES, LANES)], x_ref.at[b, pl.ds(k, n)],
                x_s.at[2 * part_no + i, b],
            )
            for i, (k, n) in enumerate(ranges[part_no])
        ]

    def deliver(b):
        return pltpu.make_async_copy(
            out_ref.at[b], out_hbm.at[:, pl.ds(b * LANES, LANES)], out_s.at[b]
        )

    for copy in small:
        copy.start()
    for part_no in range(2):
        for b in range(blocks):
            for copy in fetch(part_no, b):
                copy.start()
    for copy in small:
        copy.wait()

    land = jnp.full((LANES, cols), -1.0, jnp.float32)
    coded = jnp.where(mask_ref[...] > 0, class_ref[...], -1).astype(jnp.float32)
    for r in range(rows):
        code[1 + first + sgn * r] = jnp.broadcast_to(coded[r : r + 1, :], (LANES, cols))

    @pl.when(jnp.logical_not(has_up))
    def _():
        code[0] = land
        for b in range(blocks):
            for q in (q0, q1):
                q[b, :, 0:2] = jnp.zeros((dirs, 2, LANES, cols), jnp.float32)

    @pl.when(jnp.logical_not(has_down))
    def _():
        code[rows + 1] = land
        for b in range(blocks):
            for q in (q0, q1):
                q[b, :, rows + 2 : rows + 3] = jnp.zeros((dirs, 1, LANES, cols), jnp.float32)

    pl.semaphore_wait(barrier, groups - 1 + has_down.astype(jnp.int32) + has_up.astype(jnp.int32))

    def remote(src, dst, ssem, rsem, target):
        return pltpu.make_async_remote_copy(
            src_ref=src, dst_ref=dst, send_sem=ssem, recv_sem=rsem, device_id=target,
            device_id_type=MESH,
        )

    code_copies = (
        remote(code.at[rows], code.at[0], code_s.at[0], code_r.at[0], (me, down)),
        remote(code.at[1], code.at[rows + 1], code_s.at[1], code_r.at[1], (me, up)),
    )
    parts = ((0, 4), (4, dirs - 4))

    def halo(q, ssem, rsem, part_no, b):
        start, count = parts[part_no]
        ks = pl.ds(start, count)
        return (
            remote(
                q.at[b, ks, pl.ds(rows, 2)], q.at[b, ks, pl.ds(0, 2)],
                ssem.at[part_no, b, 0], rsem.at[part_no, b, 0], (me, down),
            ),
            remote(
                q.at[b, ks, pl.ds(2, 1)], q.at[b, ks, pl.ds(rows + 2, 1)],
                ssem.at[part_no, b, 1], rsem.at[part_no, b, 1], (me, up),
            ),
        )

    def start(copies):
        pl.when(has_down)(copies[0].start)
        pl.when(has_up)(copies[1].start)

    def wait_recv(copies):
        pl.when(has_up)(copies[0].wait_recv)
        pl.when(has_down)(copies[1].wait_recv)

    def wait_send(copies):
        pl.when(has_down)(copies[0].wait_send)
        pl.when(has_up)(copies[1].wait_send)

    start(code_copies)

    def place(p, part_no):
        return p + (p // 2) * (dirs - 4) if part_no == 0 else p - 2

    def load(part_no):
        lo, count = parts[part_no]

        def block(b):
            for copy in fetch(part_no, b):
                copy.wait()

            def one(p, _):
                k = place(p, part_no)
                tile = x_ref[b, k]
                tile = jnp.swapaxes(tile, 0, 1)
                for r in range(rows):
                    j = first + sgn * r
                    q0[b, p, 2 + j] = jnp.where(code[1 + j] >= 0.0, tile[r], 0.0)
                return 0

            lax.fori_loop(lo, lo + count, one, 0)
            start(halo(q0, h0_s, h0_r, part_no, b))

        return block

    def shifts(west):
        ahead, back = (1, cols - 1) if west else (cols - 1, 1)
        return (lambda v: pltpu.roll(v, ahead, 1)), (lambda v: pltpu.roll(v, back, 1))

    def prepare(west):
        nxt, _ = shifts(west)
        own = lax.broadcasted_iota(jnp.int32, (freqs, freqs), 0)
        other = lax.broadcasted_iota(jnp.int32, (freqs, freqs), 1)
        for level in range(depths + 1):
            line = table_ref[level : level + 1, :] if level < depths else gain_ref[...]
            spread = jnp.where(own == other, jnp.broadcast_to(line, (freqs, freqs)), 0.0)
            column = jnp.sum(spread, axis=1, keepdims=True)
            lanes[level] = jnp.broadcast_to(column, (freqs, cols))

        def block(b, _):
            for j in range(rows + 2):
                now = code[j]
                value = jnp.zeros((LANES, cols), jnp.float32)
                for level in range(depths):
                    value = jnp.where(now == float(level), lanes[level, pl.ds(b * LANES, LANES)], value)
                speed[j] = value
            for j in range(rows):
                value = speed[1 + j]
                along[b, j] = jnp.minimum(value, nxt(value))
            for j in range(rows + 1):
                across[b, j] = jnp.minimum(speed[j], speed[j + 1])
            return 0

        lax.fori_loop(0, blocks, block, 0)

    def substep(west, src, b, p, k, write):
        nxt, prv = shifts(west)
        cosine = jnp.abs(circle_ref[me * dirs + k])
        sine = jnp.abs(circle_ref[all_dirs + 1 + me * dirs + k])
        behind = src[b, p, 1] - src[b, p, 0]
        cell = src[b, p, 1]
        flux_in = None
        for i in range(rows + 1):
            after = src[b, p, i + 2]
            ahead = after - cell
            flux = upwind(*scaled(across[b, i], sine), cell, ahead, behind)
            if i > 0:
                step = nxt(cell) - cell
                fx = upwind(*scaled(along[b, i - 1], cosine), cell, step, prv(step))
                write(i - 1, cell - (fx - prv(fx)) - (flux - flux_in))
            flux_in = flux
            behind = ahead
            cell = after

    def first_pass(west, part_no):
        lo, count = parts[part_no]

        def block(b):
            wait_recv(halo(q0, h0_s, h0_r, part_no, b))

            def one(p, _):
                def write(j, value):
                    q1[b, p, 2 + j] = value

                substep(west, q0, b, p, place(p, part_no), write)
                return 0

            lax.fori_loop(lo, lo + count, one, 0)
            start(halo(q1, h1_s, h1_r, part_no, b))

        return block

    half = rows // 2

    def exchange(b, h):
        at = pl.ds(h * half, half)
        return (
            remote(
                q2.at[b, pl.ds(dirs - 2, 2), at], zlo.at[b, :, at],
                z_s.at[b, h, 0], z_r.at[b, h, 0], (right, sp),
            ),
            remote(
                q2.at[b, pl.ds(0, 2), at], zhi.at[b, :, at],
                z_s.at[b, h, 1], z_r.at[b, h, 1], (left, sp),
            ),
        )

    def second_pass(west, part_no):
        lo, count = parts[part_no]

        def block(b):
            wait_recv(halo(q1, h1_s, h1_r, part_no, b))

            def one(p, _):
                k = place(p, part_no)

                def write(j, value):
                    q2[b, k, first + sgn * j] = value

                substep(west, q1, b, p, k, write)
                return 0

            lax.fori_loop(lo, lo + count, one, 0)
            if part_no == 0:
                for h in range(2):
                    for copy in exchange(b, h):
                        copy.start()

        return block

    def both(fn):
        @pl.when(westward == 0)
        def _():
            fn(False)

        @pl.when(westward == 1)
        def _():
            fn(True)

    load(0)(0)
    wait_recv(code_copies)

    def stage(west):
        prepare(west)
        jobs = ((1, load(0)), (0, first_pass(west, 0)), (-1, second_pass(west, 0)), (0, load(1)))

        def step(s, _):
            for lag, job in jobs:

                @pl.when(jnp.logical_and(s + lag >= 0, s + lag < blocks))
                def _():
                    job(s + lag)

            return 0

        lax.fori_loop(0, blocks + 1, step, 0)

        def inner(s, _):
            pl.when(s < blocks)(lambda: first_pass(west, 1)(s))
            pl.when(s > 0)(lambda: second_pass(west, 1)(s - 1))
            return 0

        lax.fori_loop(0, blocks + 1, inner, 0)

    for face in range(dirs + 1):
        face_c = circle_ref[2 * (all_dirs + 1) + me * dirs + face]
        face_s = circle_ref[3 * (all_dirs + 1) + me * dirs + face]
        rate = face_s * slope_ref[0] - face_c * slope_ref[1]
        rate = jnp.where(mask_ref[...] > 0, rate, 0.0)
        for r in range(rows):
            turn[face, r] = jnp.broadcast_to(rate[r : r + 1, :], (LANES, cols))

    both(stage)

    acc[...] = jnp.zeros(acc.shape, jnp.float32)

    def refract(b, _):
        gain = lanes[depths, pl.ds(b * LANES, LANES)]
        place_f = b * LANES + lax.broadcasted_iota(jnp.int32, (LANES, cols), 0)
        ratio = jnp.exp((place_f.astype(jnp.float32) - 0.5 * (freqs - 1)) * math.log(1.1))
        weight = ratio * (1.0 / weight_sum)

        def row(r, _):
            def wave(k):
                if k < 0:
                    return zlo[b, k + 2, r]
                if k >= dirs:
                    return zhi[b, k - dirs, r]
                return q2[b, k, r]

            total = jnp.zeros((LANES, cols), jnp.float32)
            before, here, after = wave(-2), wave(-1), wave(0)
            d_left, d_mid = here - before, after - here
            flux_in = None
            for face in range(dirs + 1):
                beyond = wave(face + 1)
                d_right = beyond - after
                courant = gain * turn[face, r]
                size = jnp.abs(courant)
                positive = courant >= 0.0
                bend = d_mid + (1.0 / 3.0 + size * (1.0 / 3.0)) * (
                    jnp.where(positive, d_left, d_right) - d_mid
                )
                bend = bend * (0.5 - 0.5 * size)
                flux = courant * jnp.where(positive, here + bend, after - bend)
                if face > 0:
                    value = here - (flux - flux_in)
                    q3[face - 1, r] = value
                    total = total + value
                flux_in = flux
                here, after = after, beyond
                d_left, d_mid = d_mid, d_right
            total = total * weight
            acc[0, r] += total
            acc[1, r] += total * ratio
            return 0

        def piece(h, _):
            for copy in exchange(b, h):
                copy.wait_recv()
            lax.fori_loop(h * half, (h + 1) * half, row, 0)
            return 0

        lax.fori_loop(0, 2, piece, 0)

        def put(k, _):
            out_ref[b, k] = jnp.swapaxes(q3[k], 0, 1)
            return 0

        lax.fori_loop(0, dirs, put, 0)
        deliver(b).start()
        return 0

    lax.fori_loop(0, blocks, refract, 0)

    for m in range(2):
        part[m] = jnp.sum(acc[m], axis=1)
    sums = [
        remote(part, peers.at[step - 1], e_s.at[step - 1], e_r.at[step - 1],
               (lax.rem(me + step, groups), sp))
        for step in range(1, groups)
    ]
    for copy in sums:
        copy.start()

    wait_send(code_copies)

    def drain(b, _):
        for part_no in range(2):
            wait_send(halo(q0, h0_s, h0_r, part_no, b))
            wait_send(halo(q1, h1_s, h1_r, part_no, b))
        for h in range(2):
            for copy in exchange(b, h):
                copy.wait_send()
        deliver(b).wait()
        return 0

    lax.fori_loop(0, blocks, drain, 0)
    total = part[...]
    for step, copy in enumerate(sums):
        copy.wait()
        total = total + peers[step]
    sums_ref[...] = total


def sources(
    dims, circle_ref, q_hbm, sums_ref, wind_ref, mask_ref, out_hbm, factor, q_ref, out_ref, in_s, out_s
):
    dirs, all_dirs, freqs = dims
    ratios = ratio_list(freqs)

    def fetch(k):
        return pltpu.make_async_copy(q_hbm.at[k], q_ref.at[k], in_s.at[k])

    def deliver(k):
        return pltpu.make_async_copy(out_ref.at[k], out_hbm.at[k], out_s.at[k])

    for k in range(dirs):
        fetch(k).start()
    energy, moment = sums_ref[0], sums_ref[1]
    mean_freq = moment / jnp.maximum(energy, 0.25)
    steepness = energy * mean_freq * mean_freq / 4.0
    strength = 0.25 * (steepness * steepness / jnp.maximum(mean_freq, 0.5))
    wet = mask_ref[...].astype(jnp.float32)
    for f in range(freqs):
        factor[f] = wet / (1.0 + (ratios[f] * ratios[f]) * strength)

    def one(k, _):
        fetch(k).wait()
        at = lax.axis_index("comp") * dirs + k
        projected = wind_ref[0] * circle_ref[at] + wind_ref[1] * circle_ref[all_dirs + 1 + at]
        for f in range(freqs):
            growth = 0.2 * jnp.maximum(projected * ratios[f] - 1.0, 0.0)
            out_ref[k, f] = q_ref[k, f] * (1.0 + growth) * factor[f]
        deliver(k).start()
        return 0

    lax.fori_loop(0, dirs, one, 0)
    for k in range(dirs):
        deliver(k).wait()


def local(spectrum, sea_mask, depth_class, speed_table, depth_slope, turn_gain, wind_vector):
    dirs, freqs, rows, cols = spectrum.shape
    groups = lax.axis_size("comp")
    spaces = lax.axis_size("space")
    assert groups % 4 == 0 and freqs % LANES == 0 and dirs > 4 and rows % 2 == 0
    all_dirs = dirs * groups
    blocks = freqs // LANES
    angles = jnp.asarray(circle(all_dirs))
    vmem = pl.BlockSpec(memory_space=pltpu.VMEM)
    smem = pl.BlockSpec(memory_space=pltpu.SMEM)
    hbm = pl.BlockSpec(memory_space=pl.ANY)
    f32 = jnp.float32
    tile = (LANES, cols)
    dma = pltpu.SemaphoreType.DMA
    waves, sums = pl.pallas_call(
        functools.partial(kernel, (groups, spaces, dirs, blocks, rows, cols)),
        out_shape=(
            jax.ShapeDtypeStruct(spectrum.shape, f32),
            jax.ShapeDtypeStruct((2, rows, cols), f32),
        ),
        in_specs=[smem] + [hbm] * 6,
        out_specs=(hbm, vmem),
        scratch_shapes=[
            pltpu.VMEM((blocks, dirs, LANES, rows, cols), f32),
            pltpu.VMEM((rows, cols), jnp.int32),
            pltpu.VMEM((rows, cols), jnp.int32),
            pltpu.VMEM((2, rows, cols), f32),
            pltpu.VMEM(speed_table.shape, f32),
            pltpu.VMEM((1, freqs), f32),
            pltpu.VMEM((blocks, dirs, LANES, rows, cols), f32),
            dma((5,)), dma((3, blocks)), dma((blocks,)),
            pltpu.VMEM((rows + 2,) + tile, f32),
            pltpu.VMEM((speed_table.shape[0] + 1, freqs, cols), f32),
            pltpu.VMEM((rows + 2,) + tile, f32),
            pltpu.VMEM((blocks, rows) + tile, f32),
            pltpu.VMEM((blocks, rows + 1) + tile, f32),
            pltpu.VMEM((blocks, dirs, rows + 3) + tile, f32),
            pltpu.VMEM((blocks, dirs, rows + 3) + tile, f32),
            pltpu.VMEM((blocks, dirs, rows) + tile, f32),
            pltpu.VMEM((blocks, 2, rows) + tile, f32),
            pltpu.VMEM((blocks, 2, rows) + tile, f32),
            pltpu.VMEM((dirs + 1, rows) + tile, f32),
            pltpu.VMEM((dirs, rows) + tile, f32),
            pltpu.VMEM((2, rows) + tile, f32),
            pltpu.VMEM((2, rows, cols), f32),
            pltpu.VMEM((groups - 1, 2, rows, cols), f32),
            dma((2,)), dma((2,)),
            dma((2, blocks, 2)), dma((2, blocks, 2)),
            dma((2, blocks, 2)), dma((2, blocks, 2)),
            dma((blocks, 2, 2)), dma((blocks, 2, 2)),
            dma((groups - 1,)), dma((groups - 1,)),
        ],
        compiler_params=pltpu.CompilerParams(
            collective_id=0, has_side_effects=True, vmem_limit_bytes=60 * 1024 * 1024
        ),
    )(
        angles, spectrum, sea_mask, depth_class, depth_slope, speed_table,
        turn_gain.reshape(1, freqs),
    )

    block = pltpu.VMEM((dirs, freqs, rows, cols), f32)
    return pl.pallas_call(
        functools.partial(sources, (dirs, all_dirs, freqs)),
        out_shape=jax.ShapeDtypeStruct(spectrum.shape, f32),
        in_specs=[smem, hbm, vmem, vmem, vmem],
        out_specs=hbm,
        scratch_shapes=[
            pltpu.VMEM((freqs, rows, cols), f32), block, block, dma((dirs,)), dma((dirs,)),
        ],
        compiler_params=pltpu.CompilerParams(vmem_limit_bytes=60 * 1024 * 1024),
    )(angles, waves, sums, wind_vector, sea_mask)


def solution(mesh):
    in_specs = (
        P("comp", None, "space", None),
        P("space", None),
        P("space", None),
        P(),
        P(None, "space", None),
        P(),
        P(None, "space", None),
    )
    out_specs = P("comp", None, "space", None)
    return jax.shard_map(local, mesh=mesh, in_specs=in_specs, out_specs=out_specs, check_vma=False)
```
